512 devices in a mesh: ta: 64 (over x, y, core), gz: 8 (over z).
Axes of the slice: x: 4, y: 8, z: 8, core: 2. Of those that a mesh axis runs over, the one named last changes fastest.
Arguments:
- residual: float32 [64, 16, 256, 256], P('ta', 'gz'), may hold values from -8 to 8
Outputs:
- correction: float32 [64, 16, 256, 256], P('ta', 'gz')
The draws below stay inside these ranges and needn't reach their ends.
All inputs are finite; a program needn't handle non-finite values.
Results may differ from the reference program's by a relative error of at most 0.0003.
Values sent between devices are 32-bit elements; how exact they have to be, the bound alone decides.
A program may use at most 64 MiB of HBM per device.

```python
import math
from functools import partial
import jax
import jax.numpy as jnp
from jax import lax

NX = 256
NY = 256
CHEB = 4
STEPS = 64
NZ = 16


def draw_residual(key, part):
    key = jax.random.fold_in(key, 11)
    rough = jax.random.normal(key, (STEPS, NZ, NY, NX), jnp.float32)
    values = rough
    return jnp.clip(values, -8.0, 8.0)


def setup_inputs(seed: int = 0) -> dict:
    streams_of = jax.random.split(jax.random.key(seed), 2)
    return {
        "residual": draw_residual(jax.random.fold_in(streams_of[1], 71), 0),
    }


ALPHA = 0.1
SPREAD = 0.75
MASS_TAPS = (1.0 / 120, 26.0 / 120, 66.0 / 120, 26.0 / 120, 1.0 / 120)
STIFF_TAPS = (-1.0 / 6, -1.0 / 3, 1.0, -1.0 / 3, -1.0 / 6)


def along(padded, taps, axis, length):
    total = taps[0] * lax.slice_in_dim(padded, 0, length, axis=axis)
    for offset in range(1, 5):
        total = total + taps[offset] * lax.slice_in_dim(padded, offset, offset + length, axis=axis)
    return total


def pad_local(values, axis):
    widths = [(0, 0)] * values.ndim
    widths[axis] = (2, 2)
    return jnp.pad(values, widths)


def stiffness(values, pad_depth, pad_rows):
    half = values.shape[0]
    depth = values.shape[1]
    height = values.shape[2]
    breadth = values.shape[3]
    deep = pad_depth(values)
    mass_z = along(deep, MASS_TAPS, 1, depth)
    stiff_z = along(deep, STIFF_TAPS, 1, depth)
    both = pad_rows(jnp.concatenate([mass_z, stiff_z], axis=0))
    mass_part = both[:half]
    stiff_part = both[half:]
    mass_zy = along(mass_part, MASS_TAPS, 2, height)
    stiff_y = along(mass_part, STIFF_TAPS, 2, height)
    mass_y_kz = along(stiff_part, MASS_TAPS, 2, height)
    first = along(pad_local(mass_zy, 3), STIFF_TAPS, 3, breadth)
    second = along(pad_local(stiff_y + mass_y_kz, 3), MASS_TAPS, 3, breadth)
    return first + second


def lump(position, total):
    edge = jnp.where((position == 0) | (position == total - 1), 27.0 / 120, 0.0)
    near = jnp.where((position == 1) | (position == total - 2), 1.0 / 120, 0.0)
    return (1.0 - edge - near).astype(jnp.float32)


def shift_pair(frequency, length):
    radius = ALPHA ** (1.0 / length)
    phase = frequency * (2.0 * math.pi / length)
    return (1.0 - radius * jnp.cos(phase), radius * jnp.sin(phase))


def times_pair(first, second):
    return (first[0] * second[0] - first[1] * second[1], first[0] * second[1] + first[1] * second[0])


def divide_pair(top, bottom):
    norm_sq = bottom[0] * bottom[0] + bottom[1] * bottom[1]
    return ((top[0] * bottom[0] + top[1] * bottom[1]) / norm_sq, (top[1] * bottom[0] - top[0] * bottom[1]) / norm_sq)


def scalar_times(pair, values):
    return jnp.stack([pair[0] * values[0] - pair[1] * values[1], pair[0] * values[1] + pair[1] * values[0]])


def chebyshev(rhs, lumped, shift, stiff_fn):
    center = (shift[0] + SPREAD, shift[1])
    sigma = (center[0] / SPREAD, center[1] / SPREAD)
    ratio = divide_pair((1.0, 0.0), sigma)
    current = rhs
    update = scalar_times(divide_pair((1.0, 0.0), center), current / lumped)
    solution = jnp.zeros_like(rhs)
    for sweep in range(CHEB):
        solution = solution + update
        if sweep + 1 < CHEB:
            image = scalar_times(shift, lumped * update) + stiff_fn(update)
            current = current - image
            following = divide_pair((1.0, 0.0), (2.0 * sigma[0] - ratio[0], 2.0 * sigma[1] - ratio[1]))
            carried = scalar_times(times_pair(following, ratio), update)
            update = carried + scalar_times((2.0 * following[0] / SPREAD, 2.0 * following[1] / SPREAD), current / lumped)
            ratio = following
    return solution


def reference(residual):
    order = jnp.arange(STEPS).astype(jnp.float32)
    scale = jnp.exp(order * (math.log(ALPHA) / STEPS)).reshape(STEPS, 1, 1, 1)
    spectrum = jnp.fft.fft(residual * scale, axis=0)
    lumped = (lump(jnp.arange(NZ), NZ)[:, None, None] * lump(jnp.arange(NY), NY)[None, :, None]
              * lump(jnp.arange(NX), NX)[None, None, :])

    def local_stiff(values):
        return stiffness(values, partial(pad_local, axis=1), partial(pad_local, axis=2))

    def solve_one(item):
        real_part, imag_part, frequency = item
        rhs = jnp.stack([real_part, imag_part])
        return chebyshev(rhs, lumped, shift_pair(frequency, STEPS), local_stiff)

    solved = lax.map(solve_one, (spectrum.real.astype(jnp.float32), spectrum.imag.astype(jnp.float32), order))
    back = jnp.fft.ifft(solved[:, 0] + 1j * solved[:, 1], axis=0).real.astype(jnp.float32)
    return back * (1.0 / scale)
```

```python
import functools
import math

import jax
import jax.numpy as jnp
import numpy as np
from jax import lax
from jax.experimental import pallas as pl
from jax.experimental.pallas import tpu as pltpu
from jax.sharding import PartitionSpec as P

ALPHA = 0.1
SPREAD = 0.75
CHEB = 4
STEPS = 64
MESH = pl.DeviceIdType.MESH
NORM = 6.0 * 120.0 * 120.0
MIDDLE = 0.75


def power_tables():
    freq = np.arange(STEPS)
    shift = 1.0 - ALPHA ** (1.0 / STEPS) * np.exp(-2j * np.pi * freq / STEPS)
    center = shift + SPREAD
    sigma = center / SPREAD
    left = np.zeros((CHEB, STEPS), complex)
    left[0] = 1.0
    update = left / center
    total = np.zeros_like(left)
    ratio = 1.0 / sigma
    for sweep in range(CHEB):
        total = total + update
        if sweep + 1 < CHEB:
            raised = MIDDLE * update
            raised[1:] += update[:-1]
            left = left - (shift * update + raised)
            following = 1.0 / (2.0 * sigma - ratio)
            update = following * ratio * update + (2.0 * following / SPREAD) * left
            ratio = following
    n = np.arange(STEPS)
    phase = np.exp(2j * np.pi * ((n[:, None] - n[None, :])[..., None] * freq % STEPS) / STEPS)
    growth = ALPHA ** ((n[None, :] - n[:, None]) / STEPS)
    return [np.real(phase @ total[k]) / STEPS * growth for k in range(CHEB)]


def mixing_table():
    table = np.zeros((CHEB, 2, STEPS, 2, STEPS), np.float32)
    for k, matrix in enumerate(power_tables()):
        for plane in range(2):
            table[k, plane, :, plane, :] = (matrix.T * NORM).astype(np.float32)
    table = table.reshape(CHEB * 2 * STEPS, 2 * STEPS)
    high = table.astype(jnp.bfloat16)
    low = (table - high.astype(np.float32)).astype(jnp.bfloat16)
    return np.concatenate([high, low], axis=1)


def group_transpose(tiles):
    group = lax.broadcasted_iota(jnp.int32, tiles[0].shape, 1) // 16
    turned = [pltpu.roll(t, 16 * i, 1) if i else t for i, t in enumerate(tiles)]
    out = []
    for b in range(8):
        picked = turned[0]
        for i in range(1, 8):
            picked = jnp.where(group == (b + i) % 8, turned[i], picked)
        out.append(pltpu.roll(picked, 128 - 16 * b, 1) if b else picked)
    return out


def chip_x(xa, xb):
    return 2 * xa + (xa + xb) % 2


def inverse_lump(position, total):
    end = (position == 0) | (position == total - 1)
    near = (position == 1) | (position == total - 2)
    return jnp.where(end, np.float32(120.0 / 93.0), jnp.where(near, np.float32(120.0 / 119.0), np.float32(1.0)))


def kernel(x_ref, g_ref, o_ref, xin, s1, r1, e, u3, ob, s2, r2, table, in_sem, out_sem, s_sem, r_sem, hs_sem, hr_sem, plane_sem):
    me = lax.axis_index("ta")
    mz = lax.axis_index("gz")
    mx, my, mc = me // 16, (me // 2) % 8, me % 2
    xa = mx // 2
    xb = ((mx + 1) // 2) % 2
    cy = 15 * xa + (1 - 2 * xa) * my
    bx = 15 * xb + (1 - 2 * xb) * mz
    by = 2 * cy + mc
    mine = by * 16 + bx

    halves = [slice(128 * h, 128 * h + 128) for h in range(2)]
    fetches = [pltpu.make_async_copy(x_ref.at[:, halves[h]], xin.at[h], in_sem.at[h]) for h in range(2)]
    for fetch in fetches:
        fetch.start()

    barrier = pltpu.get_barrier_semaphore()
    for d in range(1, 8):
        pl.semaphore_signal(barrier, inc=1, device_id=(me, (mz + d) % 8), device_id_type=MESH)

    def greet(d, carry):
        pl.semaphore_signal(barrier, inc=1, device_id=((me + d) % 64, mz), device_id_type=MESH)
        return carry

    lax.fori_loop(1, 64, greet, 0)

    for h in range(2):
        fetches[h].wait()
        for zz in range(2):
            tiles = [xin[h, pl.ds(zz * 256 + i, 32, stride=8), :] for i in range(8)]
            for b, tile in enumerate(group_transpose(tiles)):
                s1[pl.ds(2 * (8 * h + b) + zz, 32, stride=32), :] = tile

    pl.semaphore_wait(barrier, 70)
    for d in range(1, 8):
        pl.semaphore_signal(plane_sem, inc=1, device_id=(me, (mz + d) % 8), device_id_type=MESH)
    pl.semaphore_wait(plane_sem, 7)

    columns = [(mz + d) % 8 for d in range(8)]

    def spread(start):
        def some(dx, dy, itself):
            tx, ty = (mx + dx) % 4, (my + dy) % 8
            ya = tx // 2
            yb = ((tx + 1) // 2) % 2
            row = 2 * (15 * ya + (1 - 2 * ya) * ty)
            for dc in range(2):
                tc = (mc + dc) % 2
                t = tx * 16 + ty * 2 + tc
                first = (row + tc) * 16 + 15 * yb
                for dz in range(8):
                    if itself and dc == 0 and dz == 0:
                        continue
                    start(t, columns[dz], first + (1 - 2 * yb) * columns[dz])

        def body(i, carry):
            some(i % 4, i // 4, False)
            return carry

        some(0, 0, True)
        lax.fori_loop(1, 32, body, 0)

    place = (mz * 64 + me) * 2

    def send_patch(t, tz, patch):
        pltpu.make_async_remote_copy(
            s1.at[pl.ds(2 * patch, 2)], r1.at[pl.ds(place, 2)], s_sem.at[0], r_sem.at[0],
            device_id=(t, tz), device_id_type=MESH,
        ).start()

    spread(send_patch)
    r1[pl.ds(place, 2), :] = s1[pl.ds(2 * mine, 2), :]

    def fill(y, carry):
        rows = lax.broadcasted_iota(jnp.int32, (128, 128), 0)
        lane = lax.broadcasted_iota(jnp.int32, (128, 128), 1)
        z = 2 * (rows % 8) + lane // 64
        x = bx * 16 + rows // 8
        ypos = jnp.full((128, 128), by * 8 + y, jnp.int32)
        table[y] = inverse_lump(z, 16) * inverse_lump(x, 256) * inverse_lump(ypos, 256) * np.float32(1.0 / NORM)
        return carry

    lax.fori_loop(0, 8, fill, 0)

    pltpu.make_async_copy(s1.at[pl.ds(0, 1022)], r1.at[pl.ds(0, 1022)], r_sem.at[0]).wait()

    for g in range(8):
        pair = [r1[pl.ds(g * 128 + zz, 64, stride=2), :] for zz in range(2)]
        turned = jnp.concatenate(pair, axis=0).T
        for y in range(8):
            scale = table[y, pl.ds(g, 16, stride=8), :]
            e[0, 2 + y, pl.ds(16 + g, 16, stride=8), :] = turned[16 * y : 16 * y + 16] * scale

    def neighbour(dy, dx):
        ny, nx = (by + 32 + dy) % 32, (bx + 16 + dx) % 16
        ncy, nc = ny // 2, ny % 2
        ya, yb = ncy // 8, nx // 8
        ty = 15 * ya + (1 - 2 * ya) * ncy
        tz = 15 * yb + (1 - 2 * yb) * nx
        return (chip_x(ya, yb) * 16 + ty * 2 + nc, tz)

    sides = [(-1, -1), (-1, 1), (1, -1), (1, 1), (0, -1), (0, 1), (-1, 0), (1, 0)]
    source_y = {-1: (2, 2), 0: (2, 8), 1: (8, 2)}
    source_x = {-1: (16, 16), 0: (16, 128), 1: (128, 16)}
    target_y = {-1: (10, 2), 0: (2, 8), 1: (0, 2)}
    target_x = {-1: (144, 16), 0: (16, 128), 1: (0, 16)}
    targets = [neighbour(dy, dx) for dy, dx in sides]

    def rim(k):
        copies = []
        for j, (dy, dx) in enumerate(sides):
            copy = pltpu.make_async_remote_copy(
                e.at[k, pl.ds(*source_y[dy]), pl.ds(*source_x[dx])],
                e.at[k, pl.ds(*target_y[dy]), pl.ds(*target_x[dx])],
                hs_sem.at[k, j], hr_sem.at[k, j], device_id=targets[j], device_id_type=MESH,
            )
            copy.start()
            copies.append(copy)
        return copies

    sub = lax.broadcasted_iota(jnp.int32, (8, 8, 128), 1)
    first_plane = lax.broadcasted_iota(jnp.int32, (8, 8, 128), 2) < 64

    def above(v):
        return jnp.where(sub < 7, pltpu.roll(v, 7, 1), 0.0)

    def below(v):
        return jnp.where(sub > 0, pltpu.roll(v, 1, 1), 0.0)

    def apply(k):
        def body(i, carry):
            y, half = i // 2, i % 2
            at = pl.multiple_of(half * 64, 64)
            rows = [e[k, y + j, pl.ds(at, 96), :].reshape(12, 8, 128) for j in range(5)]
            one, two = rows[1] + rows[3], rows[0] + rows[4]
            by_ = 6.0 * rows[2] - 2.0 * one - two
            ay = 66.0 * rows[2] + 26.0 * one + two
            one, two = ay[1:9] + ay[3:11], ay[0:8] + ay[4:12]
            mass = 66.0 * ay[2:10] + 26.0 * one + two
            stiff = 6.0 * ay[2:10] - 2.0 * one - two
            one, two = by_[1:9] + by_[3:11], by_[0:8] + by_[4:12]
            stiff = stiff + 66.0 * by_[2:10] + 26.0 * one + two
            c0 = 66.0 * stiff + 6.0 * mass
            c1 = pltpu.roll(26.0 * stiff - 2.0 * mass, 64, 2)
            c2 = stiff - mass
            out = c0 + c1 + jnp.where(first_plane, below(c1), above(c1)) + above(c2) + below(c2)
            out = out.reshape(64, 128) * table[y, pl.ds(at, 64), :] - MIDDLE * rows[2][2:10].reshape(64, 128)
            if k < 2:
                e[k + 1, 2 + y, pl.ds(16 + at, 64), :] = out
            else:
                u3[y, pl.ds(at, 64), :] = out
            return carry

        lax.fori_loop(0, 16, body, 0)

    flying = []
    for k in range(3):
        copies = rim(k)
        for copy in copies:
            copy.wait_recv()
        flying += copies

        @pl.when(by == 0)
        def _(k=k):
            e[k, 0:2] = jnp.zeros((2, 160, 128), jnp.float32)

        @pl.when(by == 31)
        def _(k=k):
            e[k, 10:12] = jnp.zeros((2, 160, 128), jnp.float32)

        @pl.when(bx == 0)
        def _(k=k):
            e[k, :, 0:16] = jnp.zeros((12, 16, 128), jnp.float32)

        @pl.when(bx == 15)
        def _(k=k):
            e[k, :, 144:160] = jnp.zeros((12, 16, 128), jnp.float32)

        apply(k)

    def mix(y, carry):
        parts = [e[k, 2 + y, 16:144, :] for k in range(3)] + [u3[y]]
        values = jnp.concatenate(parts, axis=1)
        high = values.astype(jnp.bfloat16)
        low = (values - high.astype(jnp.float32)).astype(jnp.bfloat16)
        wide = jnp.dot(high, g_ref[...], preferred_element_type=jnp.float32)
        narrow = jnp.dot(low, g_ref[:, 0:128], preferred_element_type=jnp.float32)
        ob[pl.ds(pl.multiple_of(y * 128, 128), 128), :] = wide[:, 0:128] + (wide[:, 128:256] + narrow)
        return carry

    lax.fori_loop(0, 8, mix, 0)

    for g in range(8):
        turned = ob[pl.ds(g, 128, stride=8), :].T
        for zz in range(2):
            s2[pl.ds(g * 128 + zz, 64, stride=2), :] = turned[64 * zz : 64 * zz + 64]

    def send_step(t, tz, patch):
        pltpu.make_async_remote_copy(
            s2.at[pl.ds((tz * 64 + t) * 2, 2)], r2.at[pl.ds(2 * mine, 2)], s_sem.at[1], r_sem.at[1],
            device_id=(t, tz), device_id_type=MESH,
        ).start()

    spread(send_step)
    r2[pl.ds(2 * mine, 2), :] = s2[pl.ds(place, 2), :]
    pltpu.make_async_copy(s2.at[pl.ds(0, 1022)], r2.at[pl.ds(0, 1022)], r_sem.at[1]).wait()

    stores = []
    for h in range(2):
        for zz in range(2):
            tiles = [r2[pl.ds(2 * (8 * h + b) + zz, 32, stride=32), :] for b in range(8)]
            for i, tile in enumerate(group_transpose(tiles)):
                xin[h, pl.ds(zz * 256 + i, 32, stride=8), :] = tile
        store = pltpu.make_async_copy(xin.at[h], o_ref.at[:, halves[h]], out_sem.at[h])
        store.start()
        stores.append(store)
    for store in stores:
        store.wait()

    for copy in flying:
        copy.wait_send()
    for j in range(2):
        pltpu.make_async_copy(s1.at[pl.ds(0, 1022)], r1.at[pl.ds(0, 1022)], s_sem.at[j]).wait()


def on_device(residual):
    vmem = functools.partial(pltpu.VMEM, dtype=jnp.float32)
    dma = pltpu.SemaphoreType.DMA
    out = pl.pallas_call(
        kernel,
        out_shape=jax.ShapeDtypeStruct((512, 256), jnp.float32),
        in_specs=[pl.BlockSpec(memory_space=pl.ANY), pl.BlockSpec(memory_space=pltpu.VMEM)],
        out_specs=pl.BlockSpec(memory_space=pl.ANY),
        scratch_shapes=[
            vmem((2, 512, 128)),
            vmem((1024, 128)),
            vmem((1024, 128)),
            vmem((3, 12, 160, 128)),
            vmem((8, 128, 128)),
            vmem((1024, 128)),
            vmem((1024, 128)),
            vmem((1024, 128)),
            vmem((8, 128, 128)),
            dma((2,)),
            dma((2,)),
            dma((2,)),
            dma((2,)),
            dma((3, 8)),
            dma((3, 8)),
            pltpu.SemaphoreType.REGULAR,
        ],
        compiler_params=pltpu.CompilerParams(
            collective_id=0, has_side_effects=True, vmem_limit_bytes=40 << 20
        ),
        name="circulant_apply",
    )(residual.reshape(512, 256), jnp.asarray(mixing_table()))
    return out.reshape(residual.shape)


def solution(mesh):
    placed = P("ta", "gz", None, None)
    return jax.shard_map(on_device, mesh=mesh, in_specs=(placed,), out_specs=placed, check_vma=False)
```

```python
import functools
import math

import jax
import jax.numpy as jnp
import numpy as np
from jax import lax
from jax.experimental import pallas as pl
from jax.experimental.pallas import tpu as pltpu
from jax.sharding import PartitionSpec as P

ALPHA = 0.1
SPREAD = 0.75
CHEB = 4
STEPS = 64
MESH = pl.DeviceIdType.MESH
NORM = 6.0 * 120.0 * 120.0
MIDDLE = 0.75
FORWARD = ((0, 1, 7, 2, 6, 3, 5, 4), (0, 1, 7, 2, 6, 3, 5, 4))
BACK = ((0, 4, 3, 5, 2, 6, 1, 7), (4, 3, 5, 2, 6, 1, 7, 0))


def power_tables():
    freq = np.arange(STEPS)
    shift = 1.0 - ALPHA ** (1.0 / STEPS) * np.exp(-2j * np.pi * freq / STEPS)
    center = shift + SPREAD
    sigma = center / SPREAD
    left = np.zeros((CHEB, STEPS), complex)
    left[0] = 1.0
    update = left / center
    total = np.zeros_like(left)
    ratio = 1.0 / sigma
    for sweep in range(CHEB):
        total = total + update
        if sweep + 1 < CHEB:
            raised = MIDDLE * update
            raised[1:] += update[:-1]
            left = left - (shift * update + raised)
            following = 1.0 / (2.0 * sigma - ratio)
            update = following * ratio * update + (2.0 * following / SPREAD) * left
            ratio = following
    n = np.arange(STEPS)
    phase = np.exp(2j * np.pi * ((n[:, None] - n[None, :])[..., None] * freq % STEPS) / STEPS)
    growth = ALPHA ** ((n[None, :] - n[:, None]) / STEPS)
    return [np.real(phase @ total[k]) / STEPS * growth for k in range(CHEB)]


def mixing_table():
    table = np.zeros((CHEB, 2, STEPS, 2, STEPS), np.float32)
    for k, matrix in enumerate(power_tables()):
        for plane in range(2):
            table[k, plane, :, plane, :] = (matrix.T * NORM).astype(np.float32)
    table = table.reshape(CHEB * 2 * STEPS, 2 * STEPS)
    high = table.astype(jnp.bfloat16)
    low = (table - high.astype(np.float32)).astype(jnp.bfloat16)
    return np.concatenate([high, low], axis=1)


def group_transpose(tiles):
    group = lax.broadcasted_iota(jnp.int32, tiles[0].shape, 1) // 16
    turned = [pltpu.roll(t, 16 * i, 1) if i else t for i, t in enumerate(tiles)]
    out = []
    for b in range(8):
        picked = turned[0]
        for i in range(1, 8):
            picked = jnp.where(group == (b + i) % 8, turned[i], picked)
        out.append(pltpu.roll(picked, 128 - 16 * b, 1) if b else picked)
    return out


def chip_x(xa, xb):
    return 2 * xa + (xa + xb) % 2


def inverse_lump(position, total):
    end = (position == 0) | (position == total - 1)
    near = (position == 1) | (position == total - 2)
    return jnp.where(end, np.float32(120.0 / 93.0), jnp.where(near, np.float32(120.0 / 119.0), np.float32(1.0)))


def kernel(x_ref, g_ref, o_ref, xin, s1, r1, e, u3, s2, r2, table, mixing, in_sem, out_sem, s_sem, r_sem, hs_sem, hr_sem, plane_sem):
    me = lax.axis_index("ta")
    mz = lax.axis_index("gz")
    mx, my, mc = me // 16, (me // 2) % 8, me % 2
    xa = mx // 2
    xb = ((mx + 1) // 2) % 2
    cy = 15 * xa + (1 - 2 * xa) * my
    bx = 15 * xb + (1 - 2 * xb) * mz
    by = 2 * cy + mc
    mine = by * 16 + bx

    halves = [slice(128 * h, 128 * h + 128) for h in range(2)]
    fetches = [pltpu.make_async_copy(x_ref.at[:, halves[h]], xin.at[h], in_sem.at[h]) for h in range(2)]
    for fetch in fetches:
        fetch.start()

    constants = pltpu.make_async_copy(g_ref, mixing, in_sem.at[2])
    constants.start()

    barrier = pltpu.get_barrier_semaphore()
    for d in range(1, 8):
        pl.semaphore_signal(barrier, inc=1, device_id=(me, (mz + d) % 8), device_id_type=MESH)

    def greet(d, carry):
        pl.semaphore_signal(barrier, inc=1, device_id=((me + d) % 64, mz), device_id_type=MESH)
        return carry

    lax.fori_loop(1, 64, greet, 0)

    for h in range(2):
        fetches[h].wait()
        for zz in range(2):
            tiles = [xin[h, pl.ds(zz * 256 + i, 32, stride=8), :] for i in range(8)]
            for b, tile in enumerate(group_transpose(tiles)):
                s1[pl.ds(2 * (8 * h + b) + zz, 32, stride=32), :] = tile

    pl.semaphore_wait(barrier, 70)
    for d in range(1, 8):
        pl.semaphore_signal(plane_sem.at[mz], inc=1, device_id=(me, (mz + d) % 8), device_id_type=MESH)

    cores = [mc, 1 - mc]

    def spread(start, ready, plane_order, row_order):
        for d in plane_order:
            tz = (mz + d) % 8
            ready(tz)

            def some(dx, skip, tz=tz):
                tx = (mx + dx) % 4
                ya = tx // 2
                yb = ((tx + 1) // 2) % 2
                across = 15 * yb + (1 - 2 * yb) * tz + 480 * ya
                step = 32 * (1 - 2 * ya)
                for dy in row_order:
                    ty = (my + dy) % 8
                    for dc in range(2):
                        if skip and dc == 0 and dy == 0:
                            continue
                        start(tx * 16 + ty * 2 + cores[dc], tz, across + step * ty + 16 * cores[dc])

            def body(i, carry, some=some):
                some(i, False)
                return carry

            if d == 0:
                some(0, True)
            lax.fori_loop(1 if d == 0 else 0, 4, body, 0)

    place = (mz * 64 + me) * 2

    def send_patch(t, tz, patch):
        pltpu.make_async_remote_copy(
            s1.at[pl.ds(2 * patch, 2)], r1.at[pl.ds(place, 2)], s_sem.at[0], r_sem.at[0],
            device_id=(t, tz), device_id_type=MESH,
        ).start()

    def entered(tz):
        @pl.when(tz != mz)
        def _():
            pl.semaphore_wait(plane_sem.at[tz], 1)

    spread(send_patch, entered, *FORWARD)
    r1[pl.ds(place, 2), :] = s1[pl.ds(2 * mine, 2), :]

    def fill(y, carry):
        rows = lax.broadcasted_iota(jnp.int32, (128, 128), 0)
        lane = lax.broadcasted_iota(jnp.int32, (128, 128), 1)
        z = 2 * (rows % 8) + lane // 64
        x = bx * 16 + rows // 8
        ypos = jnp.full((128, 128), by * 8 + y, jnp.int32)
        table[y] = inverse_lump(z, 16) * inverse_lump(x, 256) * inverse_lump(ypos, 256) * np.float32(1.0 / NORM)
        return carry

    lax.fori_loop(0, 8, fill, 0)
    constants.wait()

    pltpu.make_async_copy(s1.at[pl.ds(0, 1022)], r1.at[pl.ds(0, 1022)], r_sem.at[0]).wait()

    for g in range(8):
        pair = [r1[pl.ds(g * 128 + zz, 64, stride=2), :] for zz in range(2)]
        turned = jnp.concatenate(pair, axis=0).T
        for y in range(8):
            scale = table[y, pl.ds(g, 16, stride=8), :]
            e[0, 2 + y, pl.ds(16 + g, 16, stride=8), :] = turned[16 * y : 16 * y + 16] * scale

    def neighbour(dy, dx):
        ny, nx = (by + 32 + dy) % 32, (bx + 16 + dx) % 16
        ncy, nc = ny // 2, ny % 2
        ya, yb = ncy // 8, nx // 8
        ty = 15 * ya + (1 - 2 * ya) * ncy
        tz = 15 * yb + (1 - 2 * yb) * nx
        return (chip_x(ya, yb) * 16 + ty * 2 + nc, tz)

    sides = [(-1, -1), (-1, 1), (1, -1), (1, 1), (0, -1), (0, 1), (-1, 0), (1, 0)]
    source_y = {-1: (2, 2), 0: (2, 8), 1: (8, 2)}
    source_x = {-1: (16, 16), 0: (16, 128), 1: (128, 16)}
    target_y = {-1: (10, 2), 0: (2, 8), 1: (0, 2)}
    target_x = {-1: (144, 16), 0: (16, 128), 1: (0, 16)}
    targets = [neighbour(dy, dx) for dy, dx in sides]

    def rim(k):
        copies = []
        for j, (dy, dx) in enumerate(sides):
            copy = pltpu.make_async_remote_copy(
                e.at[k, pl.ds(*source_y[dy]), pl.ds(*source_x[dx])],
                e.at[k, pl.ds(*target_y[dy]), pl.ds(*target_x[dx])],
                hs_sem.at[k, j], hr_sem.at[k, j], device_id=targets[j], device_id_type=MESH,
            )
            copy.start()
            copies.append(copy)
        return copies

    sub = lax.broadcasted_iota(jnp.int32, (8, 8, 128), 1)
    first_plane = lax.broadcasted_iota(jnp.int32, (8, 8, 128), 2) < 64

    def above(v):
        return jnp.where(sub < 7, pltpu.roll(v, 7, 1), 0.0)

    def below(v):
        return jnp.where(sub > 0, pltpu.roll(v, 1, 1), 0.0)

    def apply(k, first, jump):
        def body(i, carry):
            y, half = first + i // 2 + (i // 4) * jump, i % 2
            at = pl.multiple_of(half * 64, 64)
            rows = [e[k, y + j, pl.ds(at, 96), :].reshape(12, 8, 128) for j in range(5)]
            one, two = rows[1] + rows[3], rows[0] + rows[4]
            by_ = 6.0 * rows[2] - 2.0 * one - two
            ay = 66.0 * rows[2] + 26.0 * one + two
            one, two = ay[1:9] + ay[3:11], ay[0:8] + ay[4:12]
            mass = 66.0 * ay[2:10] + 26.0 * one + two
            stiff = 6.0 * ay[2:10] - 2.0 * one - two
            one, two = by_[1:9] + by_[3:11], by_[0:8] + by_[4:12]
            stiff = stiff + 66.0 * by_[2:10] + 26.0 * one + two
            c0 = 66.0 * stiff + 6.0 * mass
            c1 = pltpu.roll(26.0 * stiff - 2.0 * mass, 64, 2)
            c2 = stiff - mass
            out = c0 + c1 + jnp.where(first_plane, below(c1), above(c1)) + above(c2) + below(c2)
            out = out.reshape(64, 128) * table[y, pl.ds(at, 64), :] - MIDDLE * rows[2][2:10].reshape(64, 128)
            if k < 2:
                e[k + 1, 2 + y, pl.ds(16 + at, 64), :] = out
            else:
                u3[y, pl.ds(at, 64), :] = out
            return carry

        lax.fori_loop(0, 8, body, 0)

    def clear(k, rows, columns):
        e[k, rows, columns] = jnp.zeros((rows.stop - rows.start, columns.stop - columns.start, 128), jnp.float32)

    flying = []
    outer = [slice(0, 2), slice(10, 12)]
    for k in range(3):
        copies = rim(k)
        flying += copies
        for copy in copies[4:6]:
            copy.wait_recv()

        @pl.when(bx == 0)
        def _(k=k):
            clear(k, slice(2, 10), slice(0, 16))

        @pl.when(bx == 15)
        def _(k=k):
            clear(k, slice(2, 10), slice(144, 160))

        apply(k, 2, 0)
        for copy in copies[6:8] + copies[0:4]:
            copy.wait_recv()

        @pl.when(bx == 0)
        def _(k=k):
            for rows in outer:
                clear(k, rows, slice(0, 16))

        @pl.when(bx == 15)
        def _(k=k):
            for rows in outer:
                clear(k, rows, slice(144, 160))

        @pl.when(by == 0)
        def _(k=k):
            clear(k, outer[0], slice(0, 160))

        @pl.when(by == 31)
        def _(k=k):
            clear(k, outer[1], slice(0, 160))

        apply(k, 0, 4)

    def mix(g):
        parts = []
        for k in range(4):
            cells = [
                e[k, 2 + y, pl.ds(16 + g, 16, stride=8), :] if k < 3 else u3[y, pl.ds(g, 16, stride=8), :]
                for y in range(8)
            ]
            parts.append(jnp.concatenate(cells, axis=0))
        values = jnp.concatenate(parts, axis=1)
        high = values.astype(jnp.bfloat16)
        low = (values - high.astype(jnp.float32)).astype(jnp.bfloat16)
        wide = jnp.dot(high, mixing[...], preferred_element_type=jnp.float32)
        narrow = jnp.dot(low, mixing[:, 0:128], preferred_element_type=jnp.float32)
        turned = (wide[:, 0:128] + (wide[:, 128:256] + narrow)).T
        for zz in range(2):
            s2[pl.ds(g * 128 + zz, 64, stride=2), :] = turned[64 * zz : 64 * zz + 64]

    def send_step(t, tz, patch):
        pltpu.make_async_remote_copy(
            s2.at[pl.ds((tz * 64 + t) * 2, 2)], r2.at[pl.ds(2 * mine, 2)], s_sem.at[1], r_sem.at[1],
            device_id=(t, tz), device_id_type=MESH,
        ).start()

    spread(send_step, mix, *BACK)
    r2[pl.ds(2 * mine, 2), :] = s2[pl.ds(place, 2), :]
    pltpu.make_async_copy(s2.at[pl.ds(0, 1022)], r2.at[pl.ds(0, 1022)], r_sem.at[1]).wait()

    stores = []
    for h in range(2):
        for zz in range(2):
            tiles = [r2[pl.ds(2 * (8 * h + b) + zz, 32, stride=32), :] for b in range(8)]
            for i, tile in enumerate(group_transpose(tiles)):
                xin[h, pl.ds(zz * 256 + i, 32, stride=8), :] = tile
        store = pltpu.make_async_copy(xin.at[h], o_ref.at[:, halves[h]], out_sem.at[h])
        store.start()
        stores.append(store)
    for store in stores:
        store.wait()

    for copy in flying:
        copy.wait_send()
    for j in range(2):
        pltpu.make_async_copy(s1.at[pl.ds(0, 1022)], r1.at[pl.ds(0, 1022)], s_sem.at[j]).wait()


def on_device(residual):
    vmem = functools.partial(pltpu.VMEM, dtype=jnp.float32)
    dma = pltpu.SemaphoreType.DMA
    out = pl.pallas_call(
        kernel,
        out_shape=jax.ShapeDtypeStruct((512, 256), jnp.float32),
        in_specs=[pl.BlockSpec(memory_space=pltpu.MemorySpace.HBM)] * 2,
        out_specs=pl.BlockSpec(memory_space=pltpu.MemorySpace.HBM),
        scratch_shapes=[
            vmem((2, 512, 128)),
            vmem((1024, 128)),
            vmem((1024, 128)),
            vmem((3, 12, 160, 128)),
            vmem((8, 128, 128)),
            vmem((1024, 128)),
            vmem((1024, 128)),
            vmem((8, 128, 128)),
            pltpu.VMEM((512, 256), jnp.bfloat16),
            dma((3,)),
            dma((2,)),
            dma((2,)),
            dma((2,)),
            dma((3, 8)),
            dma((3, 8)),
            pltpu.SemaphoreType.REGULAR((8,)),
        ],
        compiler_params=pltpu.CompilerParams(
            collective_id=0, has_side_effects=True, vmem_limit_bytes=60 << 20
        ),
        name="circulant_apply",
    )(residual.reshape(512, 256), jnp.asarray(mixing_table()))
    return out.reshape(residual.shape)


def solution(mesh):
    placed = P("ta", "gz", None, None)
    return jax.shard_map(on_device, mesh=mesh, in_specs=(placed,), out_specs=placed, check_vma=False)
```

```python
import functools
import math

import jax
import jax.numpy as jnp
import numpy as np
from jax import lax
from jax.experimental import pallas as pl
from jax.experimental.pallas import tpu as pltpu
from jax.sharding import PartitionSpec as P

ALPHA = 0.1
SPREAD = 0.75
CHEB = 4
STEPS = 64
MESH = pl.DeviceIdType.MESH
NORM = 6.0 * 120.0 * 120.0
MIDDLE = 0.75
FORWARD = (((0,), (1, 7, 2, 6), (3, 5, 4)), (0, 1, 7, 2, 6, 3, 5, 4))
BACK = (((0, 4, 3, 5), (2, 6, 1, 7)), (4, 3, 5, 2, 6, 1, 7, 0))


def power_tables():
    freq = np.arange(STEPS)
    shift = 1.0 - ALPHA ** (1.0 / STEPS) * np.exp(-2j * np.pi * freq / STEPS)
    center = shift + SPREAD
    sigma = center / SPREAD
    left = np.zeros((CHEB, STEPS), complex)
    left[0] = 1.0
    update = left / center
    total = np.zeros_like(left)
    ratio = 1.0 / sigma
    for sweep in range(CHEB):
        total = total + update
        if sweep + 1 < CHEB:
            raised = MIDDLE * update
            raised[1:] += update[:-1]
            left = left - (shift * update + raised)
            following = 1.0 / (2.0 * sigma - ratio)
            update = following * ratio * update + (2.0 * following / SPREAD) * left
            ratio = following
    n = np.arange(STEPS)
    phase = np.exp(2j * np.pi * ((n[:, None] - n[None, :])[..., None] * freq % STEPS) / STEPS)
    growth = ALPHA ** ((n[None, :] - n[:, None]) / STEPS)
    return [np.real(phase @ total[k]) / STEPS * growth for k in range(CHEB)]


def mixing_table():
    table = np.zeros((CHEB, 2, STEPS, 2, STEPS), np.float32)
    for k, matrix in enumerate(power_tables()):
        for plane in range(2):
            table[k, plane, :, plane, :] = (matrix.T * NORM).astype(np.float32)
    table = table.reshape(CHEB * 2 * STEPS, 2 * STEPS)
    high = table.astype(jnp.bfloat16)
    low = (table - high.astype(np.float32)).astype(jnp.bfloat16)
    return np.concatenate([high, low], axis=1)


def group_transpose(tiles):
    group = lax.broadcasted_iota(jnp.int32, tiles[0].shape, 1) // 16
    turned = [pltpu.roll(t, 16 * i, 1) if i else t for i, t in enumerate(tiles)]
    out = []
    for b in range(8):
        picked = turned[0]
        for i in range(1, 8):
            picked = jnp.where(group == (b + i) % 8, turned[i], picked)
        out.append(pltpu.roll(picked, 128 - 16 * b, 1) if b else picked)
    return out


def chip_x(xa, xb):
    return 2 * xa + (xa + xb) % 2


def inverse_lump(position, total):
    end = (position == 0) | (position == total - 1)
    near = (position == 1) | (position == total - 2)
    return jnp.where(end, np.float32(120.0 / 93.0), jnp.where(near, np.float32(120.0 / 119.0), np.float32(1.0)))


def kernel(x_ref, g_ref, o_ref, xin, s1, r1, e, u3, s2, r2, table, mixing, in_sem, out_sem, s_sem, r_sem, hs_sem, hr_sem, plane_sem):
    me = lax.axis_index("ta")
    mz = lax.axis_index("gz")
    mx, my, mc = me // 16, (me // 2) % 8, me % 2
    xa = mx // 2
    xb = ((mx + 1) // 2) % 2
    cy = 15 * xa + (1 - 2 * xa) * my
    bx = 15 * xb + (1 - 2 * xb) * mz
    by = 2 * cy + mc
    mine = by * 16 + bx

    halves = [slice(128 * h, 128 * h + 128) for h in range(2)]
    fetches = [pltpu.make_async_copy(x_ref.at[:, halves[h]], xin.at[h], in_sem.at[h]) for h in range(2)]
    for fetch in fetches:
        fetch.start()

    constants = pltpu.make_async_copy(g_ref, mixing, in_sem.at[2])
    constants.start()

    barrier = pltpu.get_barrier_semaphore()
    for d in range(1, 8):
        pl.semaphore_signal(barrier, inc=1, device_id=(me, (mz + d) % 8), device_id_type=MESH)

    def greet(d, carry):
        pl.semaphore_signal(barrier, inc=1, device_id=((me + d) % 64, mz), device_id_type=MESH)
        return carry

    lax.fori_loop(1, 64, greet, 0)

    for h in range(2):
        fetches[h].wait()
        for zz in range(2):
            tiles = [xin[h, pl.ds(zz * 256 + i, 32, stride=8), :] for i in range(8)]
            for b, tile in enumerate(group_transpose(tiles)):
                s1[pl.ds(2 * (8 * h + b) + zz, 32, stride=32), :] = tile

    pl.semaphore_wait(barrier, 70)
    for d in range(1, 8):
        pl.semaphore_signal(plane_sem.at[mz], inc=1, device_id=(me, (mz + d) % 8), device_id_type=MESH)

    cores = [mc, 1 - mc]

    def spread(start, ready, groups, row_order):
        for group in groups:
            planes = [(mz + d) % 8 for d in group]
            for tz in planes:
                ready(tz)

            def some(dx, skip, group=group, planes=planes):
                tx = (mx + dx) % 4
                ya = tx // 2
                yb = ((tx + 1) // 2) % 2
                across = [15 * yb + (1 - 2 * yb) * tz + 480 * ya for tz in planes]
                step = 32 * (1 - 2 * ya)
                for dy in row_order:
                    ty = (my + dy) % 8
                    for dc in range(2):
                        for d, tz, first in zip(group, planes, across):
                            if not (skip and d == dc == dy == 0):
                                start(tx * 16 + ty * 2 + cores[dc], tz, first + step * ty + 16 * cores[dc])

            def body(i, carry, some=some):
                some(i, False)
                return carry

            if 0 in group:
                some(0, True)
            lax.fori_loop(1 if 0 in group else 0, 4, body, 0)

    place = (mz * 64 + me) * 2

    def send_patch(t, tz, patch):
        pltpu.make_async_remote_copy(
            s1.at[pl.ds(2 * patch, 2)], r1.at[pl.ds(place, 2)], s_sem.at[0], r_sem.at[0],
            device_id=(t, tz), device_id_type=MESH,
        ).start()

    def entered(tz):
        @pl.when(tz != mz)
        def _():
            pl.semaphore_wait(plane_sem.at[tz], 1)

    spread(send_patch, entered, *FORWARD)
    r1[pl.ds(place, 2), :] = s1[pl.ds(2 * mine, 2), :]

    def fill(y, carry):
        rows = lax.broadcasted_iota(jnp.int32, (128, 128), 0)
        lane = lax.broadcasted_iota(jnp.int32, (128, 128), 1)
        z = 2 * (rows % 8) + lane // 64
        x = bx * 16 + rows // 8
        ypos = jnp.full((128, 128), by * 8 + y, jnp.int32)
        table[y] = inverse_lump(z, 16) * inverse_lump(x, 256) * inverse_lump(ypos, 256) * np.float32(1.0 / NORM)
        return carry

    lax.fori_loop(0, 8, fill, 0)
    constants.wait()

    pltpu.make_async_copy(s1.at[pl.ds(0, 1022)], r1.at[pl.ds(0, 1022)], r_sem.at[0]).wait()

    for g in range(8):
        pair = [r1[pl.ds(g * 128 + zz, 64, stride=2), :] for zz in range(2)]
        turned = jnp.concatenate(pair, axis=0).T
        for y in range(8):
            scale = table[y, pl.ds(g, 16, stride=8), :]
            e[0, 2 + y, pl.ds(16 + g, 16, stride=8), :] = turned[16 * y : 16 * y + 16] * scale

    def neighbour(dy, dx):
        ny, nx = (by + 32 + dy) % 32, (bx + 16 + dx) % 16
        ncy, nc = ny // 2, ny % 2
        ya, yb = ncy // 8, nx // 8
        ty = 15 * ya + (1 - 2 * ya) * ncy
        tz = 15 * yb + (1 - 2 * yb) * nx
        return (chip_x(ya, yb) * 16 + ty * 2 + nc, tz)

    sides = [(-1, -1), (-1, 1), (1, -1), (1, 1), (0, -1), (0, 1), (-1, 0), (1, 0)]
    source_y = {-1: (2, 2), 0: (2, 8), 1: (8, 2)}
    source_x = {-1: (16, 16), 0: (16, 128), 1: (128, 16)}
    target_y = {-1: (10, 2), 0: (2, 8), 1: (0, 2)}
    target_x = {-1: (144, 16), 0: (16, 128), 1: (0, 16)}
    targets = [neighbour(dy, dx) for dy, dx in sides]

    def rim(k):
        copies = []
        for j, (dy, dx) in enumerate(sides):
            copy = pltpu.make_async_remote_copy(
                e.at[k, pl.ds(*source_y[dy]), pl.ds(*source_x[dx])],
                e.at[k, pl.ds(*target_y[dy]), pl.ds(*target_x[dx])],
                hs_sem.at[k, j], hr_sem.at[k, j], device_id=targets[j], device_id_type=MESH,
            )
            copy.start()
            copies.append(copy)
        return copies

    def apply(k, first, jump, starts, width):
        shape = (width, 8, 128)
        sub = lax.broadcasted_iota(jnp.int32, shape, 1)
        first_plane = lax.broadcasted_iota(jnp.int32, shape, 2) < 64
        inside = jnp.where(first_plane, sub, 7 - sub) > 0

        def body(i, carry):
            y = first + i + (i // 2) * jump
            for x in starts:
                rows = [e[k, y + j, pl.ds(8 * x, 8 * width + 32), :].reshape(width + 4, 8, 128) for j in range(5)]
                one, two = rows[1] + rows[3], rows[0] + rows[4]
                by_ = 6.0 * rows[2] - 2.0 * one - two
                ay = 66.0 * rows[2] + 26.0 * one + two
                mid, left, right = slice(2, width + 2), slice(1, width + 1), slice(3, width + 3)
                one, two = ay[left] + ay[right], ay[0:width] + ay[4 : width + 4]
                mass = 66.0 * ay[mid] + 26.0 * one + two
                stiff = 6.0 * ay[mid] - 2.0 * one - two
                one, two = by_[left] + by_[right], by_[0:width] + by_[4 : width + 4]
                stiff = stiff + 66.0 * by_[mid] + 26.0 * one + two
                c0 = 66.0 * stiff + 6.0 * mass
                c1 = pltpu.roll(26.0 * stiff - 2.0 * mass, 64, 2)
                c2 = stiff - mass
                beyond = jnp.where(first_plane, pltpu.roll(c1, 1, 1), pltpu.roll(c1, 7, 1))
                out = c0 + c1 + jnp.where(inside, beyond, 0.0)
                out = out + jnp.where(sub < 7, pltpu.roll(c2, 7, 1), 0.0) + jnp.where(sub > 0, pltpu.roll(c2, 1, 1), 0.0)
                size = 8 * width
                out = out.reshape(size, 128) * table[y, pl.ds(8 * x, size), :] - MIDDLE * rows[2][mid].reshape(size, 128)
                if k < 2:
                    e[k + 1, 2 + y, pl.ds(16 + 8 * x, size), :] = out
                else:
                    u3[y, pl.ds(8 * x, size), :] = out
            return carry

        lax.fori_loop(0, 4, body, 0, unroll=True)

    def clear(when, k, *blocks):
        @pl.when(when)
        def _():
            for rows, columns in blocks:
                e[k, rows, columns] = jnp.zeros((rows.stop - rows.start, columns.stop - columns.start, 128), jnp.float32)

    top, middle, bottom = slice(0, 2), slice(2, 10), slice(10, 12)
    west, centre, east = slice(0, 16), slice(16, 144), slice(144, 160)
    flying = []
    for k in range(3):
        copies = rim(k)
        flying += copies
        apply(k, 2, 0, (2, 8), 6)
        for copy in copies[6:8]:
            copy.wait_recv()
        clear(by == 0, k, (top, centre))
        clear(by == 31, k, (bottom, centre))
        apply(k, 0, 4, (2, 8), 6)
        for copy in copies[4:6]:
            copy.wait_recv()
        clear(bx == 0, k, (middle, west))
        clear(bx == 15, k, (middle, east))
        apply(k, 2, 0, (0, 14), 2)
        for copy in copies[0:4]:
            copy.wait_recv()
        clear((bx == 0) | (by == 0), k, (top, west))
        clear((bx == 0) | (by == 31), k, (bottom, west))
        clear((bx == 15) | (by == 0), k, (top, east))
        clear((bx == 15) | (by == 31), k, (bottom, east))
        apply(k, 0, 4, (0, 14), 2)

    def mix(g):
        parts = []
        for k in range(4):
            cells = [
                e[k, 2 + y, pl.ds(16 + g, 16, stride=8), :] if k < 3 else u3[y, pl.ds(g, 16, stride=8), :]
                for y in range(8)
            ]
            parts.append(jnp.concatenate(cells, axis=0))
        values = jnp.concatenate(parts, axis=1)
        high = values.astype(jnp.bfloat16)
        low = (values - high.astype(jnp.float32)).astype(jnp.bfloat16)
        wide = jnp.dot(high, mixing[...], preferred_element_type=jnp.float32)
        narrow = jnp.dot(low, mixing[:, 0:128], preferred_element_type=jnp.float32)
        turned = (wide[:, 0:128] + (wide[:, 128:256] + narrow)).T
        for zz in range(2):
            s2[pl.ds(g * 128 + zz, 64, stride=2), :] = turned[64 * zz : 64 * zz + 64]

    def send_step(t, tz, patch):
        pltpu.make_async_remote_copy(
            s2.at[pl.ds((tz * 64 + t) * 2, 2)], r2.at[pl.ds(2 * mine, 2)], s_sem.at[1], r_sem.at[1],
            device_id=(t, tz), device_id_type=MESH,
        ).start()

    spread(send_step, mix, *BACK)
    r2[pl.ds(2 * mine, 2), :] = s2[pl.ds(place, 2), :]
    pltpu.make_async_copy(s2.at[pl.ds(0, 1022)], r2.at[pl.ds(0, 1022)], r_sem.at[1]).wait()

    stores = []
    for h in range(2):
        for zz in range(2):
            tiles = [r2[pl.ds(2 * (8 * h + b) + zz, 32, stride=32), :] for b in range(8)]
            for i, tile in enumerate(group_transpose(tiles)):
                xin[h, pl.ds(zz * 256 + i, 32, stride=8), :] = tile
        store = pltpu.make_async_copy(xin.at[h], o_ref.at[:, halves[h]], out_sem.at[h])
        store.start()
        stores.append(store)
    for store in stores:
        store.wait()

    for copy in flying:
        copy.wait_send()
    for j in range(2):
        pltpu.make_async_copy(s1.at[pl.ds(0, 1022)], r1.at[pl.ds(0, 1022)], s_sem.at[j]).wait()


def on_device(residual):
    vmem = functools.partial(pltpu.VMEM, dtype=jnp.float32)
    dma = pltpu.SemaphoreType.DMA
    out = pl.pallas_call(
        kernel,
        out_shape=jax.ShapeDtypeStruct((512, 256), jnp.float32),
        in_specs=[pl.BlockSpec(memory_space=pltpu.MemorySpace.HBM)] * 2,
        out_specs=pl.BlockSpec(memory_space=pltpu.MemorySpace.HBM),
        scratch_shapes=[
            vmem((2, 512, 128)),
            vmem((1024, 128)),
            vmem((1024, 128)),
            vmem((3, 12, 160, 128)),
            vmem((8, 128, 128)),
            vmem((1024, 128)),
            vmem((1024, 128)),
            vmem((8, 128, 128)),
            pltpu.VMEM((512, 256), jnp.bfloat16),
            dma((3,)),
            dma((2,)),
            dma((2,)),
            dma((2,)),
            dma((3, 8)),
            dma((3, 8)),
            pltpu.SemaphoreType.REGULAR((8,)),
        ],
        compiler_params=pltpu.CompilerParams(
            collective_id=0, has_side_effects=True, vmem_limit_bytes=60 << 20
        ),
        name="circulant_apply",
    )(residual.reshape(512, 256), jnp.asarray(mixing_table()))
    return out.reshape(residual.shape)


def solution(mesh):
    placed = P("ta", "gz", None, None)
    return jax.shard_map(on_device, mesh=mesh, in_specs=(placed,), out_specs=placed, check_vma=False)
```

```python
import functools
import math

import jax
import jax.numpy as jnp
import numpy as np
from jax import lax
from jax.experimental import pallas as pl
from jax.experimental.pallas import tpu as pltpu
from jax.sharding import PartitionSpec as P

ALPHA = 0.1
SPREAD = 0.75
CHEB = 4
STEPS = 64
MESH = pl.DeviceIdType.MESH
NORM = 6.0 * 120.0 * 120.0
MIDDLE = 0.75
FORWARD = (((0,), (1, 7, 2, 6), (3, 5, 4)), (0, 1, 7, 2, 6, 3, 5, 4))
BACK = (((0, 4, 3, 5), (2, 6, 1, 7)), (4, 3, 5, 2, 6, 1, 7, 0))


def power_tables():
    freq = np.arange(STEPS)
    shift = 1.0 - ALPHA ** (1.0 / STEPS) * np.exp(-2j * np.pi * freq / STEPS)
    center = shift + SPREAD
    sigma = center / SPREAD
    left = np.zeros((CHEB, STEPS), complex)
    left[0] = 1.0
    update = left / center
    total = np.zeros_like(left)
    ratio = 1.0 / sigma
    for sweep in range(CHEB):
        total = total + update
        if sweep + 1 < CHEB:
            raised = MIDDLE * update
            raised[1:] += update[:-1]
            left = left - (shift * update + raised)
            following = 1.0 / (2.0 * sigma - ratio)
            update = following * ratio * update + (2.0 * following / SPREAD) * left
            ratio = following
    n = np.arange(STEPS)
    phase = np.exp(2j * np.pi * ((n[:, None] - n[None, :])[..., None] * freq % STEPS) / STEPS)
    growth = ALPHA ** ((n[None, :] - n[:, None]) / STEPS)
    return [np.real(phase @ total[k]) / STEPS * growth for k in range(CHEB)]


def mixing_table():
    table = np.zeros((CHEB, 2, STEPS, 2, STEPS), np.float32)
    for k, matrix in enumerate(power_tables()):
        for plane in range(2):
            table[k, plane, :, plane, :] = (matrix.T * NORM).astype(np.float32)
    table = table.reshape(CHEB * 2 * STEPS, 2 * STEPS)
    high = table.astype(jnp.bfloat16)
    low = (table - high.astype(np.float32)).astype(jnp.bfloat16)
    return np.concatenate([high, low], axis=1)


def group_transpose(tiles):
    group = lax.broadcasted_iota(jnp.int32, tiles[0].shape, 1) // 16
    turned = [pltpu.roll(t, 16 * i, 1) if i else t for i, t in enumerate(tiles)]
    out = []
    for b in range(8):
        picked = turned[0]
        for i in range(1, 8):
            picked = jnp.where(group == (b + i) % 8, turned[i], picked)
        out.append(pltpu.roll(picked, 128 - 16 * b, 1) if b else picked)
    return out


def chip_x(xa, xb):
    return 2 * xa + (xa + xb) % 2


def inverse_lump(position, total):
    end = (position == 0) | (position == total - 1)
    near = (position == 1) | (position == total - 2)
    return jnp.where(end, np.float32(120.0 / 93.0), jnp.where(near, np.float32(120.0 / 119.0), np.float32(1.0)))


def kernel(x_ref, g_ref, o_ref, xin, s1, r1, e, u3, s2, r2, table, mixing, in_sem, out_sem, s_sem, r_sem, hs_sem, hr_sem, plane_sem):
    me = lax.axis_index("ta")
    mz = lax.axis_index("gz")
    mx, my, mc = me // 16, (me // 2) % 8, me % 2
    xa = mx // 2
    xb = ((mx + 1) // 2) % 2
    cy = 15 * xa + (1 - 2 * xa) * my
    bx = 15 * xb + (1 - 2 * xb) * mz
    by = 2 * cy + mc
    mine = by * 16 + bx

    halves = [slice(128 * h, 128 * h + 128) for h in range(2)]
    fetches = [pltpu.make_async_copy(x_ref.at[:, halves[h]], xin.at[h], in_sem.at[h]) for h in range(2)]
    for fetch in fetches:
        fetch.start()

    constants = pltpu.make_async_copy(g_ref, mixing, in_sem.at[2])
    constants.start()

    barrier = pltpu.get_barrier_semaphore()
    for d in range(1, 8):
        pl.semaphore_signal(barrier, inc=1, device_id=(me, (mz + d) % 8), device_id_type=MESH)

    def greet(d, carry):
        pl.semaphore_signal(barrier, inc=1, device_id=((me + d) % 64, mz), device_id_type=MESH)
        return carry

    lax.fori_loop(1, 64, greet, 0)

    for h in range(2):
        fetches[h].wait()
        for zz in range(2):
            tiles = [xin[h, pl.ds(zz * 256 + i, 32, stride=8), :] for i in range(8)]
            for b, tile in enumerate(group_transpose(tiles)):
                s1[pl.ds(2 * (8 * h + b) + zz, 32, stride=32), :] = tile

    pl.semaphore_wait(barrier, 70)
    for d in range(1, 8):
        pl.semaphore_signal(plane_sem.at[mz], inc=1, device_id=(me, (mz + d) % 8), device_id_type=MESH)

    cores = [mc, 1 - mc]

    def spread(start, ready, groups, row_order):
        for group in groups:
            planes = [(mz + d) % 8 for d in group]
            for tz in planes:
                ready(tz)

            def some(dx, skip, group=group, planes=planes):
                tx = (mx + dx) % 4
                ya = tx // 2
                yb = ((tx + 1) // 2) % 2
                across = [15 * yb + (1 - 2 * yb) * tz + 480 * ya for tz in planes]
                step = 32 * (1 - 2 * ya)
                for dy in row_order:
                    ty = (my + dy) % 8
                    for dc in range(2):
                        for d, tz, first in zip(group, planes, across):
                            if not (skip and d == dc == dy == 0):
                                start(tx * 16 + ty * 2 + cores[dc], tz, first + step * ty + 16 * cores[dc])

            def body(i, carry, some=some):
                some(i, False)
                return carry

            if 0 in group:
                some(0, True)
            lax.fori_loop(1 if 0 in group else 0, 4, body, 0)

    place = (mz * 64 + me) * 2

    def send_patch(t, tz, patch):
        pltpu.make_async_remote_copy(
            s1.at[pl.ds(2 * patch, 2)], r1.at[pl.ds(place, 2)], s_sem.at[0], r_sem.at[0],
            device_id=(t, tz), device_id_type=MESH,
        ).start()

    def entered(tz):
        @pl.when(tz != mz)
        def _():
            pl.semaphore_wait(plane_sem.at[tz], 1)

    spread(send_patch, entered, *FORWARD)
    r1[pl.ds(place, 2), :] = s1[pl.ds(2 * mine, 2), :]

    def fill(y, carry):
        rows = lax.broadcasted_iota(jnp.int32, (128, 128), 0)
        lane = lax.broadcasted_iota(jnp.int32, (128, 128), 1)
        z = 2 * (rows % 8) + lane // 64
        x = bx * 16 + rows // 8
        ypos = jnp.full((128, 128), by * 8 + y, jnp.int32)
        table[y] = inverse_lump(z, 16) * inverse_lump(x, 256) * inverse_lump(ypos, 256) * np.float32(1.0 / NORM)
        return carry

    lax.fori_loop(0, 8, fill, 0)
    constants.wait()

    pltpu.make_async_copy(s1.at[pl.ds(0, 1022)], r1.at[pl.ds(0, 1022)], r_sem.at[0]).wait()

    for g in range(8):
        pair = [r1[pl.ds(g * 128 + zz, 64, stride=2), :] for zz in range(2)]
        turned = jnp.concatenate(pair, axis=0).T
        for y in range(8):
            scale = table[y, pl.ds(g, 16, stride=8), :]
            e[0, 2 + y, pl.ds(16 + g, 16, stride=8), :] = turned[16 * y : 16 * y + 16] * scale

    def neighbour(dy, dx):
        ny, nx = (by + 32 + dy) % 32, (bx + 16 + dx) % 16
        ncy, nc = ny // 2, ny % 2
        ya, yb = ncy // 8, nx // 8
        ty = 15 * ya + (1 - 2 * ya) * ncy
        tz = 15 * yb + (1 - 2 * yb) * nx
        return (chip_x(ya, yb) * 16 + ty * 2 + nc, tz)

    sides = [(-1, -1), (-1, 1), (1, -1), (1, 1), (0, -1), (0, 1), (-1, 0), (1, 0)]
    source_y = {-1: (2, 2), 0: (2, 8), 1: (8, 2)}
    source_x = {-1: (16, 16), 0: (16, 128), 1: (128, 16)}
    target_y = {-1: (10, 2), 0: (2, 8), 1: (0, 2)}
    target_x = {-1: (144, 16), 0: (16, 128), 1: (0, 16)}
    targets = [neighbour(dy, dx) for dy, dx in sides]

    def rim(k):
        copies = []
        for j, (dy, dx) in enumerate(sides):
            copy = pltpu.make_async_remote_copy(
                e.at[k, pl.ds(*source_y[dy]), pl.ds(*source_x[dx])],
                e.at[k, pl.ds(*target_y[dy]), pl.ds(*target_x[dx])],
                hs_sem.at[k, j], hr_sem.at[k, j], device_id=targets[j], device_id_type=MESH,
            )
            copy.start()
            copies.append(copy)
        return copies

    def apply(k, first, jump, starts, width):
        shape = (width, 8, 128)
        sub = lax.broadcasted_iota(jnp.int32, shape, 1)
        first_plane = lax.broadcasted_iota(jnp.int32, shape, 2) < 64
        inside = jnp.where(first_plane, sub, 7 - sub) > 0

        def body(i, carry):
            y = first + i + (i // 2) * jump
            for x in starts:
                rows = [e[k, y + j, pl.ds(8 * x, 8 * width + 32), :].reshape(width + 4, 8, 128) for j in range(5)]
                one, two = rows[1] + rows[3], rows[0] + rows[4]
                by_ = 6.0 * rows[2] - 2.0 * one - two
                ay = 66.0 * rows[2] + 26.0 * one + two
                mid, left, right = slice(2, width + 2), slice(1, width + 1), slice(3, width + 3)
                one, two = ay[left] + ay[right], ay[0:width] + ay[4 : width + 4]
                mass = 66.0 * ay[mid] + 26.0 * one + two
                stiff = 6.0 * ay[mid] - 2.0 * one - two
                one, two = by_[left] + by_[right], by_[0:width] + by_[4 : width + 4]
                stiff = stiff + 66.0 * by_[mid] + 26.0 * one + two
                c0 = 66.0 * stiff + 6.0 * mass
                c1 = pltpu.roll(26.0 * stiff - 2.0 * mass, 64, 2)
                c2 = stiff - mass
                beyond = jnp.where(first_plane, pltpu.roll(c1, 1, 1), pltpu.roll(c1, 7, 1))
                out = c0 + c1 + jnp.where(inside, beyond, 0.0)
                out = out + jnp.where(sub < 7, pltpu.roll(c2, 7, 1), 0.0) + jnp.where(sub > 0, pltpu.roll(c2, 1, 1), 0.0)
                size = 8 * width
                out = out.reshape(size, 128) * table[y, pl.ds(8 * x, size), :] - MIDDLE * rows[2][mid].reshape(size, 128)
                if k < 2:
                    e[k + 1, 2 + y, pl.ds(16 + 8 * x, size), :] = out
                else:
                    u3[y, pl.ds(8 * x, size), :] = out
            return carry

        lax.fori_loop(0, 4, body, 0, unroll=True)

    def clear(when, k, *blocks):
        @pl.when(when)
        def _():
            for rows, columns in blocks:
                e[k, rows, columns] = jnp.zeros((rows.stop - rows.start, columns.stop - columns.start, 128), jnp.float32)

    top, middle, bottom = slice(0, 2), slice(2, 10), slice(10, 12)
    west, centre, east = slice(0, 16), slice(16, 144), slice(144, 160)
    flying = []
    for k in range(3):
        copies = rim(k)
        flying += copies
        apply(k, 2, 0, (2, 8), 6)
        for copy in copies[6:8]:
            copy.wait_recv()
        clear(by == 0, k, (top, centre))
        clear(by == 31, k, (bottom, centre))
        apply(k, 0, 4, (2, 8), 6)
        for copy in copies[4:6]:
            copy.wait_recv()
        clear(bx == 0, k, (middle, west))
        clear(bx == 15, k, (middle, east))
        apply(k, 2, 0, (0, 14), 2)
        for copy in copies[0:4]:
            copy.wait_recv()
        clear((bx == 0) | (by == 0), k, (top, west))
        clear((bx == 0) | (by == 31), k, (bottom, west))
        clear((bx == 15) | (by == 0), k, (top, east))
        clear((bx == 15) | (by == 31), k, (bottom, east))
        apply(k, 0, 4, (0, 14), 2)

    def mix(g):
        parts = []
        for k in range(4):
            cells = [
                e[k, 2 + y, pl.ds(16 + g, 16, stride=8), :] if k < 3 else u3[y, pl.ds(g, 16, stride=8), :]
                for y in range(8)
            ]
            parts.append(jnp.concatenate(cells, axis=0))
        values = jnp.concatenate(parts, axis=1)
        high = values.astype(jnp.bfloat16)
        low = (values - high.astype(jnp.float32)).astype(jnp.bfloat16)
        wide = jnp.dot(high, mixing[...], preferred_element_type=jnp.float32)
        narrow = jnp.dot(low, mixing[:, 0:128], preferred_element_type=jnp.float32)
        turned = (wide[:, 0:128] + (wide[:, 128:256] + narrow)).T
        for zz in range(2):
            s2[pl.ds(g * 128 + zz, 64, stride=2), :] = turned[64 * zz : 64 * zz + 64]

    def send_step(t, tz, patch):
        pltpu.make_async_remote_copy(
            s2.at[pl.ds((tz * 64 + t) * 2, 2)], r2.at[pl.ds(2 * mine, 2)], s_sem.at[1], r_sem.at[1],
            device_id=(t, tz), device_id_type=MESH,
        ).start()

    spread(send_step, mix, *BACK)
    r2[pl.ds(2 * mine, 2), :] = s2[pl.ds(place, 2), :]
    for copy in flying:
        copy.wait_send()
    for j in range(2):
        pltpu.make_async_copy(s1.at[pl.ds(0, 1022)], r1.at[pl.ds(0, 1022)], s_sem.at[j]).wait()
    pltpu.make_async_copy(s2.at[pl.ds(0, 1022)], r2.at[pl.ds(0, 1022)], r_sem.at[1]).wait()

    stores = []
    for h in range(2):
        for zz in range(2):
            tiles = [r2[pl.ds(2 * (8 * h + b) + zz, 32, stride=32), :] for b in range(8)]
            for i, tile in enumerate(group_transpose(tiles)):
                xin[h, pl.ds(zz * 256 + i, 32, stride=8), :] = tile
        store = pltpu.make_async_copy(xin.at[h], o_ref.at[:, halves[h]], out_sem.at[h])
        store.start()
        stores.append(store)
    for store in stores:
        store.wait()


def on_device(residual):
    vmem = functools.partial(pltpu.VMEM, dtype=jnp.float32)
    dma = pltpu.SemaphoreType.DMA
    out = pl.pallas_call(
        kernel,
        out_shape=jax.ShapeDtypeStruct((512, 256), jnp.float32),
        in_specs=[pl.BlockSpec(memory_space=pltpu.MemorySpace.HBM)] * 2,
        out_specs=pl.BlockSpec(memory_space=pltpu.MemorySpace.HBM),
        scratch_shapes=[
            vmem((2, 512, 128)),
            vmem((1024, 128)),
            vmem((1024, 128)),
            vmem((3, 12, 160, 128)),
            vmem((8, 128, 128)),
            vmem((1024, 128)),
            vmem((1024, 128)),
            vmem((8, 128, 128)),
            pltpu.VMEM((512, 256), jnp.bfloat16),
            dma((3,)),
            dma((2,)),
            dma((2,)),
            dma((2,)),
            dma((3, 8)),
            dma((3, 8)),
            pltpu.SemaphoreType.REGULAR((8,)),
        ],
        compiler_params=pltpu.CompilerParams(
            collective_id=0, has_side_effects=True, vmem_limit_bytes=60 << 20
        ),
        name="circulant_apply",
    )(residual.reshape(512, 256), jnp.asarray(mixing_table()))
    return out.reshape(residual.shape)


def solution(mesh):
    placed = P("ta", "gz", None, None)
    return jax.shard_map(on_device, mesh=mesh, in_specs=(placed,), out_specs=placed, check_vma=False)
```
